32 devices in a mesh: groups: 2 (over y), pool: 16 (over z, x, core), sub: 1.
Axes of the slice: x: 2, y: 2, z: 4, core: 2. Of those that a mesh axis runs over, the one named last changes fastest.
Arguments:
- query: bfloat16 [256, 8192], P(('groups', 'pool'), 'sub'), parts along dimension 0, may hold values from -5.5 to 5.5
- new_kv: bfloat16 [256, 2, 512], P(('groups', 'pool'), None, 'sub'), parts along dimension 0, may hold values from -5.5 to 5.5
- kv_cache: bfloat16 [256, 128, 2, 512], P(('groups', 'pool'), None, None, 'sub'), parts along dimension 0, may hold values from -5.5 to 5.5
- lengths: int32 [256], P(('groups', 'pool')), parts along dimension 0, may hold values from 1 to 128, 4096 in all
- o_weight: bfloat16 [4096, 8192], P('pool', 'sub'), may hold values from -0.25 to 0.25
- residual: bfloat16 [256, 4096], P(('groups', 'pool', 'sub')), parts along dimension 0, may hold values from -72 to 72
- norm_gain: bfloat16 [4096], replicated, may hold values from 0.099609375 to 1.8984375
- router_weight: bfloat16 [16, 4096], replicated, may hold values from -0.032470703 to 0.032470703
- expert_ids: int32 [256, 8], P(('groups', 'pool', 'sub')), parts along dimension 0, may hold values from 0 to 15, all different within a row; in each aligned block of 8 rows (0 to 7, 8 to 15, ...) at most 8 rows name the same one
- gate_weight: bfloat16 [16, 4096, 768], P('pool', None, 'sub'), may hold values from -0.078125 to 0.078125
- up_weight: bfloat16 [16, 4096, 768], P('pool', None, 'sub'), may hold values from -0.078125 to 0.078125
- down_weight: bfloat16 [16, 768, 4096], P('pool', 'sub'), may hold values from -0.29228357 to 0.29228357
Outputs:
- mixed: bfloat16 [256, 4096], P(('groups', 'pool', 'sub')), parts along dimension 0
The draws below stay inside these ranges and needn't reach their ends.
There are 2 independent parts, one for each index of `groups`. The reference program is written for one: setup_inputs(seed, part) draws one part's arguments, and reference() takes and returns one part's arrays. A program takes and returns all parts, laid end to end along the dimension named above; an argument that names none is the same for every part. Nothing has to cross between parts.
Inputs may be any that keep to these rules, and one draw needn't show every extreme that they name: `expert_ids`: each row names 8 different experts. Within the 8 rows of one device (aligned blocks) no expert is named more than 8 times, a bound that some block reaches. A row attends to its cache positions below its length and to its own new key; the longest row has exactly 128. The lengths of the 128 rows of each serving group sum to 4096; the whole array, over all groups, sums to that times the number of groups.
All inputs are finite; a program needn't handle non-finite values.
Results may differ from the reference program's by a relative error of at most 0.03.
Values may be sent and summed in bfloat16 or wider, within the bound.
A program may use at most 64 MiB of HBM per device.

```python
import math
import jax
import jax.numpy as jnp
import numpy as np
from jax import lax

D = 4096
QH = 64
KVH = 4
HEAD = 128
EFF = 768
TOPK = 8
ROWS_DEV = 8
LEN = 128
EXPERTS = 16
MOST = 8
ROWS = 128
N_SUB = 1


def loud_experts(key):
    order = jax.random.permutation(key, EXPERTS)
    return order < EXPERTS // 4


def feature_signs():
    feature_ids = jnp.arange(D, dtype=jnp.int32)
    return jnp.where((feature_ids * 97 + 13) % 31 < 15, 1.0, -1.0).astype(jnp.float32)


def expert_matrix(key, loud, shape, normal_scale, loud_limit):
    standard = jax.random.normal(key, shape, jnp.float32)
    even = lax.erf(standard * 0.5 ** 0.5)
    quiet_part = jnp.clip(standard, -4.0, 4.0) * normal_scale
    loud_part = even * loud_limit
    return jnp.where(loud[:, None, None], loud_part, quiet_part)


def draw_query(key, part):
    key = jax.random.fold_in(key, 1)
    result = jnp.clip(jax.random.normal(key, (ROWS, KVH, QH // KVH, HEAD), jnp.float32), -5.5, 5.5)
    return result.reshape(ROWS, QH * HEAD).astype(jnp.bfloat16)


def draw_kv_cache(key, part):
    key = jax.random.fold_in(key, 2)
    result = jnp.clip(jax.random.normal(key, (ROWS, LEN, 2, KVH, HEAD), jnp.float32), -5.5, 5.5)
    return result.reshape(ROWS, LEN, 2, KVH * HEAD).astype(jnp.bfloat16)


def draw_new_kv(key, part):
    key = jax.random.fold_in(key, 3)
    result = jnp.clip(jax.random.normal(key, (ROWS, 2, KVH, HEAD), jnp.float32), -5.5, 5.5)
    return result.reshape(ROWS, 2, KVH * HEAD).astype(jnp.bfloat16)


def draw_residual(key, part):
    key = jax.random.fold_in(key, 4)
    row_key, col_key, value_key = jax.random.split(key, 3)
    row_scale = jnp.exp(jax.random.uniform(row_key, (ROWS, 1), jnp.float32, math.log(0.4), math.log(4.0)))
    col_scale = jnp.exp(jax.random.uniform(col_key, (1, D), jnp.float32, math.log(0.4), math.log(4.0)))
    entries = jnp.clip(jax.random.normal(value_key, (ROWS, D), jnp.float32), -4.0, 4.0)
    common = 2.0 * feature_signs()[None, :]
    return ((entries * col_scale + common) * row_scale).astype(jnp.bfloat16)


def draw_router_weight(key, part):
    loud = loud_experts(key)
    key = jax.random.fold_in(key, 5)
    base_draw = jax.random.uniform(key, (EXPERTS, D), jnp.float32, -1.0, 1.0) * (2.0 * D ** (-0.5))
    lowered = jnp.where(loud, 5.0 / D, 0.0)[:, None] * feature_signs()[None, :]
    return (base_draw - lowered).astype(jnp.bfloat16)


def draw_gate_weight(key, part):
    loud = loud_experts(key)
    key = jax.random.fold_in(key, 6)
    return expert_matrix(key, loud, (EXPERTS, D, EFF), D ** (-0.5), 5.0 * D ** (-0.5)).astype(jnp.bfloat16)


def draw_up_weight(key, part):
    loud = loud_experts(key)
    key = jax.random.fold_in(key, 7)
    return expert_matrix(key, loud, (EXPERTS, D, EFF), D ** (-0.5), 5.0 * D ** (-0.5)).astype(jnp.bfloat16)


def draw_down_weight(key, part):
    loud = loud_experts(key)
    key = jax.random.fold_in(key, 8)
    return expert_matrix(key, loud, (EXPERTS, EFF, D), EFF ** (-0.5), 8.0 * EFF ** (-0.5)).astype(jnp.bfloat16)


def block_scale(rng, shape, cuts, low, high):
    level, own = 1.0, jax.random.fold_in(rng, 6)
    for axis_at, blocks in cuts:
        steps = jnp.exp(jax.random.uniform(jax.random.fold_in(own, axis_at), (blocks,), jnp.float32, low / len(cuts), high / len(cuts)))
        level = level * jnp.repeat(steps, shape[axis_at] // blocks).reshape([-1 if axis == axis_at else 1 for axis in range(len(shape))])
    return level


def length_profile(count, total, bound, slope):
    loads = [(1 << 20) // math.isqrt(rank ** slope) + 1 for rank in range(2, count + 1)]
    surplus, given = total - bound - (count - 1), [1] * (count - 1)
    while surplus > 0:
        movable = [i for i in range(count - 1) if given[i] < bound]
        mass, budget = sum([loads[i] for i in movable]), surplus
        for i in movable:
            addition = min(bound - given[i], max(1, budget * loads[i] // mass), surplus)
            given[i] = given[i] + addition
            surplus = surplus - addition
    return np.array([bound] + given)


def uneven(key, number_of, total, reach, skew):
    if number_of == 2:
        one = jax.random.randint(key, (), max(1, total - reach), min(reach, total - 1) + 1)
        return jnp.stack([one, total - one])
    sizes = jnp.asarray(length_profile(number_of, total, reach, skew), jnp.int32)
    twos = (number_of - 1) // 2
    giver, receiver = sizes[1:1 + 2 * twos:2], sizes[2:2 + 2 * twos:2]
    margin = jnp.minimum(giver - 1, reach - receiver)
    passed = jax.random.randint(jax.random.fold_in(key, 1), (twos,), 0, 1 << 20) % (margin + 1)
    sizes = sizes.at[1:1 + 2 * twos:2].set(giver - passed).at[2:2 + 2 * twos:2].set(receiver + passed)
    return sizes[jax.random.permutation(jax.random.fold_in(key, 2), number_of)]


def deal_out(key, own, number, rows, number_of, top, reach, lean):
    sequence = jax.random.permutation(key, number_of)
    heavy_load, ordinary = shares(number_of, rows * top, reach, lean, True), shares(number_of, rows * top, reach, lean, False)
    places = jnp.arange(number_of)

    def named(tallies, turn):
        used = int((tallies > 0).sum())
        fixed = max(1, used // 4)
        moved = fixed + (places - fixed + turn * (used - fixed)) % max(1, number_of - fixed)
        return jnp.zeros((number_of,), jnp.int32).at[sequence[jnp.where(places < fixed, places, moved)]].set(jnp.asarray(tallies, jnp.int32))

    tallies = jnp.where(number % 4 == 0, named(heavy_load, number // 4), named(ordinary, number - number // 4 - 1))
    mixed = jax.random.permutation(jax.random.fold_in(own, 3), number_of)
    donor, receiver = mixed[0:number_of // 2 * 2:2], mixed[1:number_of // 2 * 2:2]
    slack = jnp.minimum(tallies[donor] - 1, reach - tallies[receiver]) // 2
    slack = jnp.where((donor == sequence[0]) | (receiver == sequence[0]) | (tallies[receiver] == 0), 0, jnp.maximum(slack, 0))
    moved = jax.random.randint(jax.random.fold_in(own, 4), (number_of // 2,), 0, 1 << 20) % (slack + 1)
    tallies = tallies.at[donor].add(-moved).at[receiver].add(moved)
    members = jnp.searchsorted(jnp.cumsum(tallies), jnp.arange(rows * top), side="right").astype(jnp.int32)
    listing = members.reshape(top, rows).T
    listing = listing[jax.random.permutation(jax.random.fold_in(own, 1), rows)]
    turn = jax.random.randint(jax.random.fold_in(own, 2), (rows, 1), 0, top)
    return jnp.take_along_axis(listing, (jnp.arange(top)[None, :] + turn) % top, axis=1)


def shares(amount, total, bound, skew, full):
    loads = [(1 << 20) // math.isqrt(rank ** skew) + 1 for rank in range(1, amount + 1)]
    largest = bound if full else min(bound, max(-(-total // amount), total * loads[0] // sum(loads)))
    least = 1 if total - largest >= amount - 1 else 0
    given, spare = [largest] + [least] * (amount - 1), total - largest - least * (amount - 1)
    while spare > 0:
        candidates = [i for i in range(1, amount) if given[i] < largest] or [i for i in range(1, amount) if given[i] < bound]
        mass, left = sum([loads[i] for i in candidates]), spare
        for i in candidates:
            extra = min(bound - given[i], max(1, left * loads[i] // mass), spare)
            given[i] = given[i] + extra
            spare = spare - extra
    return np.array(given)


def centred(key, extent, deviation, most, cuts=(), kind=jnp.bfloat16):
    values = deviation * jax.random.normal(key, extent, jnp.float32)
    if cuts:
        values = values * block_scale(key, extent, cuts, -0.22, 0.18)
    return jnp.clip(values, -most, most).astype(kind)


def setup_inputs(seed: int = 0, part: int = 0) -> dict:
    splits = jax.random.split(jax.random.key(seed), 13)
    own_keys = jax.random.split(jax.random.fold_in(splits[12], part), 13)
    query = draw_query(jax.random.fold_in(jax.random.fold_in(splits[12], part), 71), part)
    new_kv = draw_new_kv(jax.random.fold_in(jax.random.fold_in(splits[12], part), 71), part)
    kv_cache = draw_kv_cache(jax.random.fold_in(jax.random.fold_in(splits[12], part), 71), part)
    lengths = uneven(own_keys[3], ROWS, ROWS * LEN // 4, LEN, 2).astype(jnp.int32)
    o_weight = centred(splits[4], (D, QH * HEAD), (QH * HEAD // 16) ** -0.5, 0.25, ((0, 16),))
    residual = draw_residual(jax.random.fold_in(jax.random.fold_in(splits[12], part), 71), part)
    norm_gain = jnp.clip(1.0 + 0.18 * jax.random.normal(splits[6], (D,), jnp.float32), 0.099609375, 1.8984375).astype(jnp.bfloat16)
    router_weight = draw_router_weight(jax.random.fold_in(splits[12], 71), part)
    expert_ids_keys = jax.random.split(jax.random.fold_in(own_keys[8], 1), ROWS // ROWS_DEV)
    expert_ids_turns = jax.random.permutation(jax.random.fold_in(own_keys[8], 3), ROWS // ROWS_DEV)
    expert_ids = jax.vmap(lambda own, number: deal_out(jax.random.fold_in(own_keys[8], 2), own, number, ROWS_DEV, EXPERTS, TOPK, MOST, 2))(expert_ids_keys, expert_ids_turns).reshape((ROWS, TOPK))
    gate_weight = draw_gate_weight(jax.random.fold_in(splits[12], 71), part)
    up_weight = draw_up_weight(jax.random.fold_in(splits[12], 71), part)
    down_weight = draw_down_weight(jax.random.fold_in(splits[12], 71), part)
    return {"query": query, "new_kv": new_kv, "kv_cache": kv_cache, "lengths": lengths, "o_weight": o_weight, "residual": residual, "norm_gain": norm_gain, "router_weight": router_weight, "expert_ids": expert_ids, "gate_weight": gate_weight, "up_weight": up_weight, "down_weight": down_weight}


norm_eps = 1e-06

def attend(query, new_kv, kv_cache, lengths):
    per_group = QH // KVH
    queries = query.reshape(ROWS, KVH, per_group, HEAD).astype(jnp.float32)
    cached_keys = kv_cache[:, :, 0].reshape(ROWS, LEN, KVH, HEAD).astype(jnp.float32)
    cached_values = kv_cache[:, :, 1].reshape(ROWS, LEN, KVH, HEAD).astype(jnp.float32)
    new_key = new_kv[:, 0].reshape(ROWS, KVH, HEAD).astype(jnp.float32)
    new_value = new_kv[:, 1].reshape(ROWS, KVH, HEAD).astype(jnp.float32)
    score_scale = HEAD ** (-0.5)
    scores = jnp.einsum('rgqd,rjgd->rgqj', queries, cached_keys) * score_scale
    own_score = jnp.einsum('rgqd,rgd->rgq', queries, new_key) * score_scale
    visible = jnp.arange(LEN, dtype=jnp.int32)[None, :] < lengths[:, None]
    scores = jnp.where(visible[:, None, None, :], scores, jnp.float32(-1e+30))
    row_max = jnp.maximum(lax.optimization_barrier(jnp.max(scores, axis=-1)), own_score)
    weights = jnp.exp(scores - row_max[..., None])
    own_weight = jnp.exp(own_score - row_max)
    denominator = lax.optimization_barrier(jnp.sum(weights, axis=-1)) + own_weight
    attn_probs = (weights / denominator[..., None]).astype(jnp.bfloat16)
    own_prob = (own_weight / denominator).astype(jnp.bfloat16)
    attended = jnp.einsum('rgqj,rjgd->rgqd', attn_probs.astype(jnp.float32), cached_values)
    attended = attended + own_prob.astype(jnp.float32)[..., None] * new_value[:, :, None, :]
    return attended.astype(jnp.bfloat16).reshape(ROWS, QH * HEAD)

def reference(query, new_kv, kv_cache, lengths, o_weight, residual, norm_gain, router_weight, expert_ids, gate_weight, up_weight, down_weight):
    attended = attend(query, new_kv, kv_cache, lengths)
    projected = jnp.dot(attended, o_weight.T, preferred_element_type=jnp.float32)
    hidden = residual.astype(jnp.float32) + projected
    mean_square = lax.optimization_barrier(jnp.mean(hidden * hidden, axis=-1, keepdims=True))
    normed = (hidden * lax.rsqrt(mean_square + norm_eps) * norm_gain.astype(jnp.float32)).astype(jnp.bfloat16)
    logits = jnp.dot(normed, router_weight.T, preferred_element_type=jnp.float32)
    chosen = jnp.take_along_axis(logits, expert_ids, axis=1)
    raised = jnp.exp(chosen)
    route_weight = raised / lax.optimization_barrier(jnp.sum(raised, axis=1, keepdims=True))
    blocks = ROWS // ROWS_DEV
    onehot = expert_ids[:, :, None] == jnp.arange(EXPERTS, dtype=jnp.int32)[None, None, :]
    member = lax.optimization_barrier(jnp.sum(onehot.astype(jnp.int32), axis=1))
    member_blocks = member.reshape(blocks, ROWS_DEV, EXPERTS)
    rank_blocks = jnp.cumsum(member_blocks, axis=1) - member_blocks
    slot_hit = (member_blocks[..., None] == 1) & (rank_blocks[..., None] == jnp.arange(MOST, dtype=jnp.int32))
    local_rows = jnp.arange(ROWS_DEV, dtype=jnp.int32)[None, :, None, None]
    slot_row = lax.optimization_barrier(jnp.sum(jnp.where(slot_hit, local_rows, 0), axis=1)).astype(jnp.int32)
    slot_live = jnp.any(slot_hit, axis=1)
    block_base = (jnp.arange(blocks, dtype=jnp.int32) * ROWS_DEV)[:, None, None]
    slot_index = (slot_row + block_base).astype(jnp.int32)

    def one_expert(operands):
        index_list, live_list, gate_one, up_one, down_one = operands
        gathered = normed[index_list.reshape(-1)]
        gathered = jnp.where(live_list.reshape(-1)[:, None], gathered, jnp.zeros_like(gathered))
        gate_proj = jnp.dot(gathered, gate_one, preferred_element_type=jnp.float32)
        up_proj = jnp.dot(gathered, up_one, preferred_element_type=jnp.float32)
        inner_act = (jax.nn.silu(gate_proj) * up_proj).astype(jnp.bfloat16)
        inner_blocks = inner_act.reshape(-1, N_SUB, EFF // N_SUB).astype(jnp.float32)
        down_blocks = down_one.reshape(N_SUB, EFF // N_SUB, D).astype(jnp.float32)
        half_out = jnp.einsum('nth,thd->ntd', inner_blocks, down_blocks).astype(jnp.bfloat16)
        expert_out = lax.optimization_barrier(jnp.sum(half_out.astype(jnp.float32), axis=1))
        return expert_out.reshape(blocks, MOST, D)
    operands = (jnp.moveaxis(slot_index, 1, 0), jnp.moveaxis(slot_live, 1, 0), gate_weight, up_weight, down_weight)
    outputs = lax.map(one_expert, operands)
    rank_rows = rank_blocks.reshape(ROWS, EXPERTS)
    slot_of = jnp.take_along_axis(rank_rows, expert_ids, axis=1).astype(jnp.int32)
    block_ids = (jnp.arange(ROWS, dtype=jnp.int32) // ROWS_DEV)[:, None]
    picked = outputs[expert_ids, block_ids, slot_of]
    mixed = lax.optimization_barrier(jnp.sum(route_weight[:, :, None] * picked, axis=1))
    return mixed.astype(jnp.bfloat16)
```

```python
import functools

import jax
import jax.numpy as jnp
from jax import lax
from jax.experimental import pallas as pl
from jax.experimental.pallas import tpu as pltpu
from jax.sharding import PartitionSpec as P

QH = 64
KVH = 4
HEAD = 128
TOPK = 8


norm_eps = 1e-06


def attend(query, new_kv, kv_cache, lengths):
    rows_att = query.shape[0]
    cache_len = kv_cache.shape[1]
    groups = kv_cache.shape[3] // HEAD
    per_group = QH // KVH
    queries = query.reshape(rows_att, groups, per_group, HEAD)
    cached_keys = kv_cache[:, :, 0].reshape(rows_att, cache_len, groups, HEAD)
    cached_values = kv_cache[:, :, 1].reshape(rows_att, cache_len, groups, HEAD)
    new_key = new_kv[:, 0].reshape(rows_att, groups, HEAD)
    new_value = new_kv[:, 1].reshape(rows_att, groups, HEAD)
    score_scale = HEAD ** (-0.5)
    scores = (
        jnp.einsum("rgqd,rjgd->rgqj", queries, cached_keys, preferred_element_type=jnp.float32)
        * score_scale
    )
    own_score = (
        jnp.einsum("rgqd,rgd->rgq", queries, new_key, preferred_element_type=jnp.float32)
        * score_scale
    )
    visible = jnp.arange(cache_len, dtype=jnp.int32)[None, :] < lengths[:, None]
    scores = jnp.where(visible[:, None, None, :], scores, jnp.float32(-1e30))
    row_max = jnp.maximum(jnp.max(scores, axis=-1), own_score)
    weights = jnp.exp(scores - row_max[..., None])
    own_weight = jnp.exp(own_score - row_max)
    denominator = jnp.sum(weights, axis=-1) + own_weight
    attn_probs = (weights / denominator[..., None]).astype(jnp.bfloat16)
    own_prob = (own_weight / denominator).astype(jnp.bfloat16)
    attended = jnp.einsum(
        "rgqj,rjgd->rgqd", attn_probs, cached_values, preferred_element_type=jnp.float32
    )
    attended = (
        attended
        + own_prob.astype(jnp.float32)[..., None] * new_value.astype(jnp.float32)[:, :, None, :]
    )
    return attended.astype(jnp.bfloat16).reshape(rows_att, -1)


def per_device(
    query,
    new_kv,
    kv_cache,
    lengths,
    o_weight,
    residual,
    norm_gain,
    router_weight,
    expert_ids,
    gate_weight,
    up_weight,
    down_weight,
):
    pool_size = lax.axis_size("pool")
    sub_size = lax.axis_size("sub")
    rows_dev = residual.shape[0]
    width = residual.shape[1]
    col_count = o_weight.shape[0]
    experts = router_weight.shape[0]
    attended = attend(query, new_kv, kv_cache, lengths)
    partial_value = lax.dot_general(
        lax.all_gather(attended, "pool", axis=0, tiled=True),
        o_weight,
        (((1,), (1,)), ((), ())),
        preferred_element_type=jnp.float32,
    )
    exchanged = lax.all_to_all(
        partial_value.astype(jnp.bfloat16), ("pool", "sub"), split_axis=0, concat_axis=1, tiled=True
    ).astype(partial_value.dtype)
    projected = jnp.sum(
        exchanged.reshape(rows_dev, pool_size, sub_size, col_count), axis=2
    ).reshape(rows_dev, width)
    hidden = residual.astype(jnp.float32) + projected
    mean_square = jnp.mean(hidden * hidden, axis=-1, keepdims=True)
    normed = (hidden * lax.rsqrt(mean_square + norm_eps) * norm_gain.astype(jnp.float32)).astype(
        jnp.bfloat16
    )
    logits = lax.dot_general(
        normed, router_weight, (((1,), (1,)), ((), ())), preferred_element_type=jnp.float32
    )
    onehot = expert_ids[:, :, None] == jnp.arange(experts, dtype=jnp.int32)[None, None, :]
    chosen = jnp.sum(jnp.where(onehot, logits[:, None, :], 0.0), axis=2)
    raised = jnp.exp(chosen)
    route_weight = raised / jnp.sum(raised, axis=1, keepdims=True)
    weight_full = jnp.sum(jnp.where(onehot, route_weight[:, :, None], 0.0), axis=1)
    capacity = min(rows_dev, max(2, 2 * rows_dev * TOPK // pool_size))
    member = jnp.sum(onehot.astype(jnp.int32), axis=1)
    rank_in_block = jnp.cumsum(member, axis=0) - member
    slot_ids = jnp.arange(capacity, dtype=jnp.int32)
    selector = (member.T[:, None, :] == 1) & (
        rank_in_block.T[:, None, :] == slot_ids[None, :, None]
    )
    combine_coef = jnp.where(selector, weight_full.T[:, None, :], 0.0)
    selector_bf = selector.astype(jnp.bfloat16)
    sending = jnp.einsum(
        "emr,rd->emd", selector_bf, normed, preferred_element_type=jnp.float32
    ).astype(jnp.bfloat16)
    doubled = jnp.broadcast_to(sending[:, None], (experts, sub_size, capacity, width)).reshape(
        experts * sub_size, capacity, width
    )
    arrived = lax.all_to_all(doubled, ("pool", "sub"), split_axis=0, concat_axis=0, tiled=True)
    item_count = arrived.shape[-2]
    flat_rows = arrived.reshape(-1, arrived.shape[-1])
    gate_proj = jnp.dot(flat_rows, gate_weight[0], preferred_element_type=jnp.float32)
    up_proj = jnp.dot(flat_rows, up_weight[0], preferred_element_type=jnp.float32)
    inner_act = (jax.nn.silu(gate_proj) * up_proj).astype(jnp.bfloat16)
    half_out = jnp.dot(inner_act, down_weight[0], preferred_element_type=jnp.float32).astype(
        jnp.bfloat16
    )
    returned = lax.all_to_all(
        half_out.reshape(-1, item_count, half_out.shape[-1]),
        ("pool", "sub"),
        split_axis=0,
        concat_axis=0,
        tiled=True,
    )
    merged = jnp.sum(
        returned.reshape(experts, sub_size, capacity, width).astype(jnp.float32), axis=1
    )
    mixed = jnp.einsum("emr,emd->rd", combine_coef, merged, precision=lax.Precision.HIGHEST)
    return mixed.astype(jnp.bfloat16)


AG_CHUNKS = 2
RS_CHUNKS = 4


def contract(a, b, dims):
    return lax.dot_general(a, b, ((dims[0], dims[1]), ((), ())), preferred_element_type=jnp.float32)


def fold(value):
    half = value.shape[1] // 2
    return jnp.concatenate([value[:, :half], value[:, half:]], axis=0)


def fused_kernel(
    query, new_kv, kv, lengths, o_weight, residual, norm_gain, router, expert_ids, gate, up, down,
    out,
    kv_v, o_v, gate_v, up_v, down_v, q_s, att_s, gathered, small_out, small_in, hid, gate_acc, up_acc,
    partial, sib_out, sib_in, x_out, x_in, z_out, z_in, own_sum,
    load_sem, small_send, small_recv, ag_send, ag_recv, hid_send, hid_recv,
    sib_send, sib_recv, x_send, x_recv, z_send, z_recv,
):
    me = lax.axis_index("pool")
    core = lax.rem(me, 2)
    x = lax.rem(me // 2, 2)
    z = me // 4
    sibling = z * 4 + x * 2 + (1 - core)
    x_peer = z * 4 + (1 - x) * 2 + core

    def z_of(j):
        return lax.rem(z + j, 4)

    def same_x(j):
        return z_of(j) * 4 + x * 2 + core

    def other_x(j):
        return z_of(j) * 4 + (1 - x) * 2 + core

    def flip(index):
        return index - core + (1 - core)

    def remote(src, dst, send_sem, recv_sem, target):
        return pltpu.make_async_remote_copy(
            src_ref=src, dst_ref=dst, send_sem=send_sem, recv_sem=recv_sem,
            device_id={"pool": target}, device_id_type=pl.DeviceIdType.MESH,
        )

    barrier = pltpu.get_barrier_semaphore()
    for offset in range(1, 16):
        pl.semaphore_signal(
            barrier, inc=1, device_id={"pool": lax.rem(me + offset, 16)},
            device_id_type=pl.DeviceIdType.MESH,
        )

    loads = [pltpu.make_async_copy(kv.at[g], kv_v.at[g], load_sem.at[g]) for g in range(4)]
    for at, (a, b) in enumerate(((o_weight, o_v), (gate, gate_v), (up, up_v), (down, down_v))):
        loads.append(pltpu.make_async_copy(a, b, load_sem.at[4 + at]))
    for load in loads:
        load.start()

    lane = lax.broadcasted_iota(jnp.int32, (8, 128), 1)
    member = jnp.zeros((8, 128), jnp.float32)
    for k in range(TOPK):
        member = member + (expert_ids[:, k : k + 1] == lane).astype(jnp.float32)
    member_pad = jnp.concatenate([member, jnp.zeros_like(member)], axis=0).astype(jnp.bfloat16)
    res = residual[...].astype(jnp.float32)
    for d in range(16):
        small_out[d, 0:16, :] = fold(res[:, d * 256 : (d + 1) * 256]).astype(jnp.bfloat16)
        small_out[d, 16:32, :] = member_pad
    small_in[me] = small_out[me]

    q_all = query[...].astype(jnp.float32)
    for h in range(QH):
        q_s[h] = q_all[:, h * 128 : (h + 1) * 128]

    pl.semaphore_wait(barrier, 15)

    def small_copy(offset):
        target = lax.rem(me + offset, 16)
        return remote(
            small_out.at[target], small_in.at[me], small_send.at[offset], small_recv.at[me], target
        )

    def small_arrival(offset):
        source = lax.rem(me + offset, 16)
        return remote(
            small_out.at[source], small_in.at[source], small_send.at[offset], small_recv.at[source], source
        )

    for offset in range(1, 16):
        small_copy(offset).start()

    score_scale = HEAD ** (-0.5)
    position = lax.broadcasted_iota(jnp.int32, (16, 256), 1)
    is_key = lax.rem(position, 2) == 0
    position = position // 2

    def attend_one(r, g, slot):
        q_f = q_s[pl.ds(g * 16, 16), r, :]
        both = kv_v[g, r]
        scores = contract(q_f.astype(jnp.bfloat16), both, ((1,), (1,))) * score_scale
        key = new_kv[r, g : g + 1, :]
        value = new_kv[r, 4 + g : 5 + g, :]
        own = jnp.sum(q_f * key, axis=1, keepdims=True) * score_scale
        scores = jnp.where(is_key & (position < lengths[r]), scores, jnp.float32(-1e30))
        top = jnp.maximum(jnp.max(scores, axis=1, keepdims=True), own)
        weights = jnp.exp(scores - top)
        own_weight = jnp.exp(own - top)
        scale = 1.0 / (jnp.sum(weights, axis=1, keepdims=True) + own_weight)
        probs = pltpu.roll(weights * scale, 1, 1).astype(jnp.bfloat16)
        own_prob = (own_weight * scale).astype(jnp.bfloat16).astype(jnp.float32)
        att_s[pl.ds(slot * 16, 16), r, :] = contract(probs, both, ((1,), (0,))) + own_prob * value

    def gather_ops(buf, send_sem, recv_sem):
        def send(source, target, n):
            return remote(buf.at[source], buf.at[source], send_sem.at[n], recv_sem.at[source], target)

        own = [send(me, same_x(j), j - 1) for j in (1, 2, 3)]
        own += [send(me, x_peer, 3), send(me, sibling, 4)]

        def arrive(source):
            send(source, sibling, 0).wait_recv()

        def relay_z(j):
            arrive(same_x(j))
            a = send(same_x(j), x_peer, 3 + 2 * j)
            b = send(same_x(j), sibling, 4 + 2 * j)
            a.start()
            b.start()

        def relay_x(j):
            arrive(other_x(j))
            send(other_x(j), sibling, 11 + j).start()

        def finish():
            for n in range(15):
                send(me, sibling, n).wait_send()

        return own, arrive, relay_z, relay_x, finish

    rings = [
        gather_ops(gathered.at[k], ag_send.at[k], ag_recv.at[k]) for k in range(AG_CHUNKS)
    ]
    for k in range(AG_CHUNKS):
        for gg in range(2):
            loads[2 * k + gg].wait()

        def rows(step, carry, k=k):
            for rr in range(4):
                for gg in range(2):
                    attend_one(step * 4 + rr, 2 * k + gg, gg)
            return carry

        lax.fori_loop(0, 2, rows, 0)
        for h in range(16):
            gathered[k, me, :, h * 128 : (h + 1) * 128] = jnp.concatenate(
                [att_s[h], att_s[16 + h]], axis=0
            ).astype(jnp.bfloat16)
        for copy in rings[k][0]:
            copy.start()

    for k in range(AG_CHUNKS):
        own, arrive, relay_z, relay_x, finish = rings[k]
        for j in (1, 2, 3):
            relay_z(j)
        for j in (0, 1, 2, 3):
            relay_x(j)
    loads[4].wait()
    total = jnp.zeros((128, 256), jnp.float32)
    for k in range(AG_CHUNKS):
        own, arrive, relay_z, relay_x, finish = rings[k]
        for j in range(4):
            arrive(flip(same_x(j)))
            arrive(flip(other_x(j)))
        left = gathered[k].reshape(256, 2048)
        for gg in range(2):
            first = k * 4096 + gg * 2048
            product = contract(left, o_v[:, first : first + 2048], ((1,), (1,)))
            total = total + product.reshape(16, 2, 8, 256)[:, gg].reshape(128, 256)

    for offset in range(1, 16):
        small_arrival(offset).wait_recv()
    pieces = small_in[:, 0:16, :].astype(jnp.float32).reshape(16, 2, 8, 128)
    res_part = jnp.concatenate(
        [pieces[:, 0].reshape(128, 128), pieces[:, 1].reshape(128, 128)], axis=1
    )
    hid[me] = (total + res_part).astype(jnp.bfloat16)

    own, arrive, relay_z, relay_x, finish_hid = gather_ops(hid, hid_send, hid_recv)
    for copy in own:
        copy.start()
    loads[5].wait()
    loads[6].wait()
    for j in (1, 2, 3):
        relay_z(j)

    def project(pair, state, first=False):
        square, logits = state
        gate_sum = up_sum = None
        for t in range(2):
            s = pair * 2 + t
            at = pl.ds(pl.multiple_of(s * 256, 256), 256)
            h = hid[s].astype(jnp.float32)
            square = square + jnp.sum(h * h, axis=1, keepdims=True)
            scaled = (h * norm_gain[:, at].astype(jnp.float32)).astype(jnp.bfloat16)
            logits = logits + contract(scaled, router[:, at], ((1,), (1,)))
            a = contract(scaled, gate_v[at, :], ((1,), (0,)))
            b = contract(scaled, up_v[at, :], ((1,), (0,)))
            gate_sum = a if gate_sum is None else gate_sum + a
            up_sum = b if up_sum is None else up_sum + b
        if first:
            gate_acc[...] = gate_sum
            up_acc[...] = up_sum
        else:
            gate_acc[...] += gate_sum
            up_acc[...] += up_sum
        return square, logits

    state = (jnp.zeros((128, 1), jnp.float32), jnp.zeros((128, 16), jnp.float32))
    for j in range(4):
        arrive(flip(same_x(j)))
        state = project(z_of(j) * 2 + x, state, first=j == 0)
        relay_x(j)
    for j in range(4):
        arrive(flip(other_x(j)))
        state = project(z_of(j) * 2 + (1 - x), state)
    square, logits = state
    inv = lax.rsqrt(square * (1.0 / 4096) + norm_eps)
    logits = logits * inv
    members = small_in[:, 16:32, :].astype(jnp.float32)[:, 0:8, :].reshape(128, 128)[:, 0:16]
    raised = jnp.where(members > 0.5, jnp.exp(logits), 0.0)
    mine = lax.broadcasted_iota(jnp.int32, (128, 16), 1) == me
    coef = jnp.sum(jnp.where(mine, raised, 0.0), axis=1, keepdims=True) / jnp.sum(
        raised, axis=1, keepdims=True
    )
    gate_proj = gate_acc[...] * inv
    inner = (gate_proj / (1.0 + jnp.exp(-gate_proj)) * (up_acc[...] * inv)).astype(jnp.bfloat16)
    loads[7].wait()

    width = 4096 // RS_CHUNKS

    def sib_copy(n):
        return remote(sib_out.at[n], sib_in.at[n], sib_send.at[n], sib_recv.at[n], sibling)

    def x_copy(n):
        return remote(x_out.at[n], x_in.at[n], x_send.at[n], x_recv.at[n], x_peer)

    def z_copy(n, j):
        return remote(
            z_out.at[n, j - 1], z_in.at[n, j - 1], z_send.at[n, j - 1], z_recv.at[n, j - 1], same_x(j)
        )

    def stage_down(n):
        product = contract(inner, down_v[:, n * width : (n + 1) * width], ((1,), (0,))) * coef
        partial[n] = product.reshape(16, 8, width)
        for chip in range(8):
            sib_out[n, chip] = fold(partial[n, chip * 2 + (1 - core)]).astype(jnp.bfloat16)
        sib_copy(n).start()

    def chip_sum(n, chip):
        return fold(partial[n, chip * 2 + core]) + sib_in[n, chip].astype(jnp.float32)

    def stage_x(n):
        sib_copy(n).wait_recv()
        for zz in range(4):
            x_out[n, zz] = chip_sum(n, zz * 2 + (1 - x)).astype(jnp.bfloat16)
        x_copy(n).start()

    def stage_z(n):
        x_copy(n).wait_recv()
        for j in range(4):
            total = chip_sum(n, z_of(j) * 2 + x) + x_in[n, z_of(j)].astype(jnp.float32)
            if j:
                z_out[n, j - 1] = total.astype(jnp.bfloat16)
                z_copy(n, j).start()
            else:
                own_sum[n] = total

    def stage_end(n):
        total = own_sum[n]
        for j in (1, 2, 3):
            z_copy(n, j).wait_recv()
            total = total + z_in[n, j - 1].astype(jnp.float32)
        out[:, n * width : (n + 1) * width] = jnp.concatenate(
            [total[0:8], total[8:16]], axis=1
        ).astype(jnp.bfloat16)

    stages = (stage_down, stage_x, stage_z, stage_end)
    for step in range(RS_CHUNKS + 3):
        for depth, stage in enumerate(stages):
            if 0 <= step - depth < RS_CHUNKS:
                stage(step - depth)

    for offset in range(1, 16):
        small_copy(offset).wait_send()
    for ring in rings:
        ring[4]()
    finish_hid()
    for n in range(RS_CHUNKS):
        sib_copy(n).wait_send()
        x_copy(n).wait_send()
        for j in (1, 2, 3):
            z_copy(n, j).wait_send()


def fused_device(
    query, new_kv, kv_cache, lengths, o_weight, residual, norm_gain, router_weight, expert_ids,
    gate_weight, up_weight, down_weight,
):
    bf16, f32 = jnp.bfloat16, jnp.float32
    dma = pltpu.SemaphoreType.DMA
    kv = kv_cache.reshape(8, 128, 2, 4, 128).transpose(3, 0, 1, 2, 4).reshape(4, 8, 256, 128)
    new = new_kv.reshape(8, 8, 128).astype(f32)
    half = 4096 // RS_CHUNKS // 2
    vmem = pl.BlockSpec(memory_space=pltpu.VMEM)
    smem = pl.BlockSpec(memory_space=pltpu.SMEM)
    hbm = pl.BlockSpec(memory_space=pl.ANY)
    return pl.pallas_call(
        fused_kernel,
        out_shape=jax.ShapeDtypeStruct((8, 4096), bf16),
        in_specs=[vmem, vmem, hbm, smem, hbm, vmem, vmem, vmem, vmem, hbm, hbm, hbm],
        out_specs=vmem,
        scratch_shapes=[
            pltpu.VMEM((4, 8, 256, 128), bf16),
            pltpu.VMEM((256, 8192), bf16),
            pltpu.VMEM((4096, 768), bf16),
            pltpu.VMEM((4096, 768), bf16),
            pltpu.VMEM((768, 4096), bf16),
            pltpu.VMEM((64, 8, 128), f32),
            pltpu.VMEM((32, 8, 128), f32),
            pltpu.VMEM((AG_CHUNKS, 16, 16, 2048), bf16),
            pltpu.VMEM((16, 32, 128), bf16),
            pltpu.VMEM((16, 32, 128), bf16),
            pltpu.VMEM((16, 128, 256), bf16),
            pltpu.VMEM((128, 768), f32),
            pltpu.VMEM((128, 768), f32),
            pltpu.VMEM((RS_CHUNKS, 16, 8, 2 * half), f32),
            pltpu.VMEM((RS_CHUNKS, 8, 16, half), bf16),
            pltpu.VMEM((RS_CHUNKS, 8, 16, half), bf16),
            pltpu.VMEM((RS_CHUNKS, 4, 16, half), bf16),
            pltpu.VMEM((RS_CHUNKS, 4, 16, half), bf16),
            pltpu.VMEM((RS_CHUNKS, 3, 16, half), bf16),
            pltpu.VMEM((RS_CHUNKS, 3, 16, half), bf16),
            pltpu.VMEM((RS_CHUNKS, 16, half), f32),
            dma((8,)),
            dma((16,)),
            dma((16,)),
            dma((AG_CHUNKS, 15)),
            dma((AG_CHUNKS, 16)),
            dma((15,)),
            dma((16,)),
            dma((RS_CHUNKS,)),
            dma((RS_CHUNKS,)),
            dma((RS_CHUNKS,)),
            dma((RS_CHUNKS,)),
            dma((RS_CHUNKS, 3)),
            dma((RS_CHUNKS, 3)),
        ],
        compiler_params=pltpu.CompilerParams(
            collective_id=0, has_side_effects=True, vmem_limit_bytes=56 * 1024 * 1024
        ),
        cost_estimate=pl.CostEstimate(
            flops=3_500_000_000, bytes_accessed=27_000_000, transcendentals=300_000
        ),
    )(
        query, new, kv, lengths, o_weight, residual, norm_gain.reshape(1, 4096), router_weight,
        expert_ids, gate_weight[0], up_weight[0], down_weight[0],
    )


def solution(mesh):
    in_specs = (
        P(("groups", "pool"), "sub"),
        P(("groups", "pool"), None, "sub"),
        P(("groups", "pool"), None, None, "sub"),
        P(("groups", "pool")),
        P("pool", "sub"),
        P(("groups", "pool", "sub"), None),
        P(),
        P(),
        P(("groups", "pool", "sub"), None),
        P("pool", None, "sub"),
        P("pool", None, "sub"),
        P("pool", "sub", None),
    )
    out_specs = P(("groups", "pool", "sub"), None)
    sizes = dict(mesh.shape)
    fused = sizes["pool"] == 16 and sizes["sub"] == 1
    return jax.shard_map(
        fused_device if fused else per_device, mesh=mesh, in_specs=in_specs, out_specs=out_specs, check_vma=False
    )
```

```python
import functools

import jax
import jax.numpy as jnp
from jax import lax
from jax.experimental import pallas as pl
from jax.experimental.pallas import tpu as pltpu
from jax.sharding import PartitionSpec as P

QH = 64
KVH = 4
HEAD = 128
TOPK = 8


norm_eps = 1e-06


def attend(query, new_kv, kv_cache, lengths):
    rows_att = query.shape[0]
    cache_len = kv_cache.shape[1]
    groups = kv_cache.shape[3] // HEAD
    per_group = QH // KVH
    queries = query.reshape(rows_att, groups, per_group, HEAD)
    cached_keys = kv_cache[:, :, 0].reshape(rows_att, cache_len, groups, HEAD)
    cached_values = kv_cache[:, :, 1].reshape(rows_att, cache_len, groups, HEAD)
    new_key = new_kv[:, 0].reshape(rows_att, groups, HEAD)
    new_value = new_kv[:, 1].reshape(rows_att, groups, HEAD)
    score_scale = HEAD ** (-0.5)
    scores = (
        jnp.einsum("rgqd,rjgd->rgqj", queries, cached_keys, preferred_element_type=jnp.float32)
        * score_scale
    )
    own_score = (
        jnp.einsum("rgqd,rgd->rgq", queries, new_key, preferred_element_type=jnp.float32)
        * score_scale
    )
    visible = jnp.arange(cache_len, dtype=jnp.int32)[None, :] < lengths[:, None]
    scores = jnp.where(visible[:, None, None, :], scores, jnp.float32(-1e30))
    row_max = jnp.maximum(jnp.max(scores, axis=-1), own_score)
    weights = jnp.exp(scores - row_max[..., None])
    own_weight = jnp.exp(own_score - row_max)
    denominator = jnp.sum(weights, axis=-1) + own_weight
    attn_probs = (weights / denominator[..., None]).astype(jnp.bfloat16)
    own_prob = (own_weight / denominator).astype(jnp.bfloat16)
    attended = jnp.einsum(
        "rgqj,rjgd->rgqd", attn_probs, cached_values, preferred_element_type=jnp.float32
    )
    attended = (
        attended
        + own_prob.astype(jnp.float32)[..., None] * new_value.astype(jnp.float32)[:, :, None, :]
    )
    return attended.astype(jnp.bfloat16).reshape(rows_att, -1)


def per_device(
    query,
    new_kv,
    kv_cache,
    lengths,
    o_weight,
    residual,
    norm_gain,
    router_weight,
    expert_ids,
    gate_weight,
    up_weight,
    down_weight,
):
    pool_size = lax.axis_size("pool")
    sub_size = lax.axis_size("sub")
    rows_dev = residual.shape[0]
    width = residual.shape[1]
    col_count = o_weight.shape[0]
    experts = router_weight.shape[0]
    attended = attend(query, new_kv, kv_cache, lengths)
    partial_value = lax.dot_general(
        lax.all_gather(attended, "pool", axis=0, tiled=True),
        o_weight,
        (((1,), (1,)), ((), ())),
        preferred_element_type=jnp.float32,
    )
    exchanged = lax.all_to_all(
        partial_value.astype(jnp.bfloat16), ("pool", "sub"), split_axis=0, concat_axis=1, tiled=True
    ).astype(partial_value.dtype)
    projected = jnp.sum(
        exchanged.reshape(rows_dev, pool_size, sub_size, col_count), axis=2
    ).reshape(rows_dev, width)
    hidden = residual.astype(jnp.float32) + projected
    mean_square = jnp.mean(hidden * hidden, axis=-1, keepdims=True)
    normed = (hidden * lax.rsqrt(mean_square + norm_eps) * norm_gain.astype(jnp.float32)).astype(
        jnp.bfloat16
    )
    logits = lax.dot_general(
        normed, router_weight, (((1,), (1,)), ((), ())), preferred_element_type=jnp.float32
    )
    onehot = expert_ids[:, :, None] == jnp.arange(experts, dtype=jnp.int32)[None, None, :]
    chosen = jnp.sum(jnp.where(onehot, logits[:, None, :], 0.0), axis=2)
    raised = jnp.exp(chosen)
    route_weight = raised / jnp.sum(raised, axis=1, keepdims=True)
    weight_full = jnp.sum(jnp.where(onehot, route_weight[:, :, None], 0.0), axis=1)
    capacity = min(rows_dev, max(2, 2 * rows_dev * TOPK // pool_size))
    member = jnp.sum(onehot.astype(jnp.int32), axis=1)
    rank_in_block = jnp.cumsum(member, axis=0) - member
    slot_ids = jnp.arange(capacity, dtype=jnp.int32)
    selector = (member.T[:, None, :] == 1) & (
        rank_in_block.T[:, None, :] == slot_ids[None, :, None]
    )
    combine_coef = jnp.where(selector, weight_full.T[:, None, :], 0.0)
    selector_bf = selector.astype(jnp.bfloat16)
    sending = jnp.einsum(
        "emr,rd->emd", selector_bf, normed, preferred_element_type=jnp.float32
    ).astype(jnp.bfloat16)
    doubled = jnp.broadcast_to(sending[:, None], (experts, sub_size, capacity, width)).reshape(
        experts * sub_size, capacity, width
    )
    arrived = lax.all_to_all(doubled, ("pool", "sub"), split_axis=0, concat_axis=0, tiled=True)
    item_count = arrived.shape[-2]
    flat_rows = arrived.reshape(-1, arrived.shape[-1])
    gate_proj = jnp.dot(flat_rows, gate_weight[0], preferred_element_type=jnp.float32)
    up_proj = jnp.dot(flat_rows, up_weight[0], preferred_element_type=jnp.float32)
    inner_act = (jax.nn.silu(gate_proj) * up_proj).astype(jnp.bfloat16)
    half_out = jnp.dot(inner_act, down_weight[0], preferred_element_type=jnp.float32).astype(
        jnp.bfloat16
    )
    returned = lax.all_to_all(
        half_out.reshape(-1, item_count, half_out.shape[-1]),
        ("pool", "sub"),
        split_axis=0,
        concat_axis=0,
        tiled=True,
    )
    merged = jnp.sum(
        returned.reshape(experts, sub_size, capacity, width).astype(jnp.float32), axis=1
    )
    mixed = jnp.einsum("emr,emd->rd", combine_coef, merged, precision=lax.Precision.HIGHEST)
    return mixed.astype(jnp.bfloat16)


AG_CHUNKS = 2
RS_CHUNKS = 4
HID_CHUNKS = 2
hid_rows = 128 // HID_CHUNKS


def contract(a, b, dims):
    return lax.dot_general(a, b, ((dims[0], dims[1]), ((), ())), preferred_element_type=jnp.float32)


def fold(value):
    half = value.shape[1] // 2
    return jnp.concatenate([value[:, :half], value[:, half:]], axis=0)


def fused_kernel(
    query, new_kv, kv, lengths, o_weight, residual, norm_gain, router, expert_ids, gate, up, down,
    out,
    kv_v, o_v, gate_v, up_v, down_v, q_s, att_s, gathered, small_out, small_in, hid, gate_acc, up_acc,
    partial, sib_out, sib_in, x_out, x_in, z_out, z_in, own_sum,
    gain_row, load_sem, small_send, small_recv, ag_send, ag_recv, hid_send, hid_recv,
    sib_send, sib_recv, x_send, x_recv, z_send, z_recv,
):
    me = lax.axis_index("pool")
    core = lax.rem(me, 2)
    x = lax.rem(me // 2, 2)
    z = me // 4
    sibling = z * 4 + x * 2 + (1 - core)
    x_peer = z * 4 + (1 - x) * 2 + core

    def z_of(j):
        return lax.rem(z + j, 4)

    def same_x(j):
        return z_of(j) * 4 + x * 2 + core

    def other_x(j):
        return z_of(j) * 4 + (1 - x) * 2 + core

    def flip(index):
        return index - core + (1 - core)

    def remote(src, dst, send_sem, recv_sem, target):
        return pltpu.make_async_remote_copy(
            src_ref=src, dst_ref=dst, send_sem=send_sem, recv_sem=recv_sem,
            device_id={"pool": target}, device_id_type=pl.DeviceIdType.MESH,
        )

    barrier = pltpu.get_barrier_semaphore()
    for offset in range(1, 16):
        pl.semaphore_signal(
            barrier, inc=1, device_id={"pool": lax.rem(me + offset, 16)},
            device_id_type=pl.DeviceIdType.MESH,
        )

    loads = [
        pltpu.make_async_copy(kv.at[:, :, :, pl.ds(g * 128, 128)], kv_v.at[g], load_sem.at[g])
        for g in range(4)
    ]
    for at, (a, b) in enumerate(((o_weight, o_v), (gate, gate_v), (up, up_v), (down, down_v))):
        loads.append(pltpu.make_async_copy(a, b, load_sem.at[4 + at]))
    for load in loads[:4]:
        load.start()

    lane = lax.broadcasted_iota(jnp.int32, (8, 128), 1)
    member = jnp.zeros((8, 128), jnp.float32)
    for k in range(TOPK):
        member = member + (expert_ids[:, k : k + 1] == lane).astype(jnp.float32)
    member_pad = jnp.concatenate([member, jnp.zeros_like(member)], axis=0).astype(jnp.bfloat16)
    res = residual[...].astype(jnp.float32)
    for d in range(16):
        small_out[d, 0:16, :] = fold(res[:, d * 256 : (d + 1) * 256]).astype(jnp.bfloat16)
        small_out[d, 16:32, :] = member_pad
    small_in[me] = small_out[me]

    q_all = query[...].astype(jnp.float32)
    for h in range(QH):
        q_s[h] = q_all[:, h * 128 : (h + 1) * 128]

    pl.semaphore_wait(barrier, 15)

    def small_copy(offset):
        target = lax.rem(me + offset, 16)
        return remote(
            small_out.at[target], small_in.at[me], small_send.at[offset], small_recv.at[me], target
        )

    def small_arrival(offset):
        source = lax.rem(me + offset, 16)
        return remote(
            small_out.at[source], small_in.at[source], small_send.at[offset], small_recv.at[source], source
        )

    for offset in range(1, 16):
        small_copy(offset).start()

    kv_rows = kv_v.reshape(4, 8, 256, 128)
    score_scale = HEAD ** (-0.5)
    position = lax.broadcasted_iota(jnp.int32, (16, 256), 1)
    is_key = lax.rem(position, 2) == 0
    position = position // 2

    def attend_group(g, slot):
        queries = [q_s[pl.ds(g * 16, 16), r, :] for r in range(8)]
        fresh = [new_kv[r, :, g * 128 : (g + 1) * 128].astype(jnp.float32) for r in range(8)]
        scores = [
            jnp.where(
                is_key & (position < lengths[r]),
                contract(queries[r].astype(jnp.bfloat16), kv_rows[g, r], ((1,), (1,))) * score_scale,
                jnp.float32(-1e30),
            )
            for r in range(8)
        ]
        scores = jnp.concatenate(scores, axis=0)
        keys = jnp.concatenate([jnp.broadcast_to(f[0:1], (16, 128)) for f in fresh], axis=0)
        own = jnp.sum(jnp.concatenate(queries, axis=0) * keys, axis=1, keepdims=True) * score_scale
        top = jnp.maximum(jnp.max(scores, axis=1, keepdims=True), own)
        weights = jnp.exp(scores - top)
        own_weight = jnp.exp(own - top)
        scale = 1.0 / (jnp.sum(weights, axis=1, keepdims=True) + own_weight)
        probs = pltpu.roll(weights * scale, 1, 1).astype(jnp.bfloat16)
        own_prob = (own_weight * scale).astype(jnp.bfloat16).astype(jnp.float32)
        results = [
            contract(probs[r * 16 : (r + 1) * 16], kv_rows[g, r], ((1,), (0,)))
            + own_prob[r * 16 : (r + 1) * 16] * fresh[r][1:2]
            for r in range(8)
        ]
        for r in range(8):
            att_s[pl.ds(slot * 16, 16), r, :] = results[r]

    def gather_ops(buf, send_sem, recv_sem):
        def send(source, target, n):
            return remote(buf.at[source], buf.at[source], send_sem.at[n], recv_sem.at[source], target)

        own = [send(me, same_x(j), j - 1) for j in (1, 2, 3)]
        own += [send(me, x_peer, 3), send(me, sibling, 4)]

        def arrive(source):
            send(source, sibling, 0).wait_recv()

        def relay_z(j):
            arrive(same_x(j))
            a = send(same_x(j), x_peer, 3 + 2 * j)
            b = send(same_x(j), sibling, 4 + 2 * j)
            a.start()
            b.start()

        def relay_x(j):
            arrive(other_x(j))
            send(other_x(j), sibling, 11 + j).start()

        def finish():
            for n in range(15):
                send(me, sibling, n).wait_send()

        return own, arrive, relay_z, relay_x, finish

    rings = [
        gather_ops(gathered.at[k], ag_send.at[k], ag_recv.at[k]) for k in range(AG_CHUNKS)
    ]
    for k in range(AG_CHUNKS):
        for gg in range(2):
            loads[2 * k + gg].wait()
        if k == 0:
            for load in loads[4:]:
                load.start()
        for gg in range(2):
            attend_group(2 * k + gg, gg)
        for h in range(16):
            gathered[k, me, :, h * 128 : (h + 1) * 128] = jnp.concatenate(
                [att_s[h], att_s[16 + h]], axis=0
            ).astype(jnp.bfloat16)
        for copy in rings[k][0]:
            copy.start()

    for ring in rings:
        for j in (1, 2, 3):
            ring[2](j)
    for ring in rings:
        for j in (0, 1, 2, 3):
            ring[3](j)
    loads[4].wait()
    total = jnp.zeros((128, 256), jnp.float32)
    for k in range(AG_CHUNKS):
        own, arrive, relay_z, relay_x, finish = rings[k]
        for j in range(4):
            arrive(flip(same_x(j)))
            arrive(flip(other_x(j)))
        left = gathered[k].reshape(256, 2048)
        for gg in range(2):
            first = k * 4096 + gg * 2048
            product = contract(left, o_v[:, first : first + 2048], ((1,), (1,)))
            total = total + product.reshape(16, 2, 8, 256)[:, gg].reshape(128, 256)

    for offset in range(1, 16):
        small_arrival(offset).wait_recv()
    pieces = small_in[:, 0:16, :].astype(jnp.float32).reshape(16, 2, 8, 128)
    res_part = jnp.concatenate(
        [pieces[:, 0].reshape(128, 128), pieces[:, 1].reshape(128, 128)], axis=1
    )
    gain_row[...] = norm_gain[...].reshape(1, 4096).astype(jnp.float32)
    hidden = (total + res_part).astype(jnp.bfloat16)
    hid_rings = [gather_ops(hid.at[k], hid_send.at[k], hid_recv.at[k]) for k in range(HID_CHUNKS)]
    for k in range(HID_CHUNKS):
        hid[k, me] = hidden[k * hid_rows : (k + 1) * hid_rows]
        for copy in hid_rings[k][0]:
            copy.start()
    loads[5].wait()
    loads[6].wait()
    for ring in hid_rings:
        for j in (1, 2, 3):
            ring[2](j)

    def project(pair, state, first=False):
        square, logits = state
        gate_sum = up_sum = None
        for t in range(2):
            s = pair * 2 + t
            at = pl.ds(pl.multiple_of(s * 256, 256), 256)
            h = jnp.concatenate([hid[k, s] for k in range(HID_CHUNKS)], axis=0).astype(jnp.float32)
            square = square + jnp.sum(h * h, axis=1, keepdims=True)
            scaled = (h * gain_row[:, at]).astype(jnp.bfloat16)
            logits = logits + contract(scaled, router[:, at], ((1,), (1,)))
            a = contract(scaled, gate_v[at, :], ((1,), (0,)))
            b = contract(scaled, up_v[at, :], ((1,), (0,)))
            gate_sum = a if gate_sum is None else gate_sum + a
            up_sum = b if up_sum is None else up_sum + b
        if first:
            gate_acc[...] = gate_sum
            up_acc[...] = up_sum
        else:
            gate_acc[...] += gate_sum
            up_acc[...] += up_sum
        return square, logits

    state = (jnp.zeros((128, 1), jnp.float32), jnp.zeros((128, 16), jnp.float32))
    for j in range(4):
        for ring in hid_rings:
            ring[1](flip(same_x(j)))
        state = project(z_of(j) * 2 + x, state, first=j == 0)
        for ring in hid_rings:
            ring[3](j)
    for j in range(4):
        for ring in hid_rings:
            ring[1](flip(other_x(j)))
        state = project(z_of(j) * 2 + (1 - x), state)
    square, logits = state
    inv = lax.rsqrt(square * (1.0 / 4096) + norm_eps)
    logits = logits * inv
    members = small_in[:, 16:32, :].astype(jnp.float32)[:, 0:8, :].reshape(128, 128)[:, 0:16]
    raised = jnp.where(members > 0.5, jnp.exp(logits), 0.0)
    mine = lax.broadcasted_iota(jnp.int32, (128, 16), 1) == me
    coef = jnp.sum(jnp.where(mine, raised, 0.0), axis=1, keepdims=True) / jnp.sum(
        raised, axis=1, keepdims=True
    )
    gate_proj = gate_acc[...] * inv
    inner = (gate_proj / (1.0 + jnp.exp(-gate_proj)) * (up_acc[...] * inv)).astype(jnp.bfloat16)
    loads[7].wait()

    width = 4096 // RS_CHUNKS

    def sib_copy(n):
        return remote(sib_out.at[n], sib_in.at[n], sib_send.at[n], sib_recv.at[n], sibling)

    def x_copy(n):
        return remote(x_out.at[n], x_in.at[n], x_send.at[n], x_recv.at[n], x_peer)

    def z_copy(n, j):
        return remote(
            z_out.at[n, j - 1], z_in.at[n, j - 1], z_send.at[n, j - 1], z_recv.at[n, j - 1], same_x(j)
        )

    def stage_down(n):
        product = contract(inner, down_v[:, n * width : (n + 1) * width], ((1,), (0,))) * coef
        partial[n] = product.reshape(16, 8, width)
        for chip in range(8):
            sib_out[n, chip] = fold(partial[n, chip * 2 + (1 - core)]).astype(jnp.bfloat16)
        sib_copy(n).start()

    def chip_sum(n, chip):
        return fold(partial[n, chip * 2 + core]) + sib_in[n, chip].astype(jnp.float32)

    def stage_x(n):
        sib_copy(n).wait_recv()
        for zz in range(4):
            x_out[n, zz] = chip_sum(n, zz * 2 + (1 - x)).astype(jnp.bfloat16)
        x_copy(n).start()

    def stage_z(n):
        x_copy(n).wait_recv()
        for j in range(4):
            total = chip_sum(n, z_of(j) * 2 + x) + x_in[n, z_of(j)].astype(jnp.float32)
            if j:
                z_out[n, j - 1] = total.astype(jnp.bfloat16)
                z_copy(n, j).start()
            else:
                own_sum[n] = total

    def stage_end(n):
        total = own_sum[n]
        for j in (1, 2, 3):
            z_copy(n, j).wait_recv()
            total = total + z_in[n, j - 1].astype(jnp.float32)
        out[:, n * width : (n + 1) * width] = jnp.concatenate(
            [total[0:8], total[8:16]], axis=1
        ).astype(jnp.bfloat16)

    for stage in (stage_down, stage_x, stage_z, stage_end):
        for n in range(RS_CHUNKS):
            stage(n)

    for offset in range(1, 16):
        small_copy(offset).wait_send()
    for ring in rings:
        ring[4]()
    for ring in hid_rings:
        ring[4]()
    for n in range(RS_CHUNKS):
        sib_copy(n).wait_send()
        x_copy(n).wait_send()
        for j in (1, 2, 3):
            z_copy(n, j).wait_send()


def fused_device(
    query, new_kv, kv_cache, lengths, o_weight, residual, norm_gain, router_weight, expert_ids,
    gate_weight, up_weight, down_weight,
):
    bf16, f32 = jnp.bfloat16, jnp.float32
    dma = pltpu.SemaphoreType.DMA
    half = 4096 // RS_CHUNKS // 2
    vmem = pl.BlockSpec(memory_space=pltpu.VMEM)
    smem = pl.BlockSpec(memory_space=pltpu.SMEM)
    hbm = pl.BlockSpec(memory_space=pl.ANY)
    return pl.pallas_call(
        fused_kernel,
        out_shape=jax.ShapeDtypeStruct((8, 4096), bf16),
        in_specs=[vmem, vmem, hbm, smem, hbm, vmem, vmem, vmem, vmem, hbm, hbm, hbm],
        out_specs=vmem,
        scratch_shapes=[
            pltpu.VMEM((4, 8, 128, 2, 128), bf16),
            pltpu.VMEM((256, 8192), bf16),
            pltpu.VMEM((4096, 768), bf16),
            pltpu.VMEM((4096, 768), bf16),
            pltpu.VMEM((768, 4096), bf16),
            pltpu.VMEM((64, 8, 128), f32),
            pltpu.VMEM((32, 8, 128), f32),
            pltpu.VMEM((AG_CHUNKS, 16, 16, 2048), bf16),
            pltpu.VMEM((16, 32, 128), bf16),
            pltpu.VMEM((16, 32, 128), bf16),
            pltpu.VMEM((HID_CHUNKS, 16, hid_rows, 256), bf16),
            pltpu.VMEM((128, 768), f32),
            pltpu.VMEM((128, 768), f32),
            pltpu.VMEM((RS_CHUNKS, 16, 8, 2 * half), f32),
            pltpu.VMEM((RS_CHUNKS, 8, 16, half), bf16),
            pltpu.VMEM((RS_CHUNKS, 8, 16, half), bf16),
            pltpu.VMEM((RS_CHUNKS, 4, 16, half), bf16),
            pltpu.VMEM((RS_CHUNKS, 4, 16, half), bf16),
            pltpu.VMEM((RS_CHUNKS, 3, 16, half), bf16),
            pltpu.VMEM((RS_CHUNKS, 3, 16, half), bf16),
            pltpu.VMEM((RS_CHUNKS, 16, half), f32),
            pltpu.VMEM((1, 4096), f32),
            dma((8,)),
            dma((16,)),
            dma((16,)),
            dma((AG_CHUNKS, 15)),
            dma((AG_CHUNKS, 16)),
            dma((HID_CHUNKS, 15)),
            dma((HID_CHUNKS, 16)),
            dma((RS_CHUNKS,)),
            dma((RS_CHUNKS,)),
            dma((RS_CHUNKS,)),
            dma((RS_CHUNKS,)),
            dma((RS_CHUNKS, 3)),
            dma((RS_CHUNKS, 3)),
        ],
        compiler_params=pltpu.CompilerParams(
            collective_id=0, has_side_effects=True, vmem_limit_bytes=56 * 1024 * 1024
        ),
        cost_estimate=pl.CostEstimate(
            flops=3_500_000_000, bytes_accessed=27_000_000, transcendentals=300_000
        ),
    )(
        query, new_kv, kv_cache, lengths, o_weight, residual, norm_gain, router_weight,
        expert_ids, gate_weight[0], up_weight[0], down_weight[0],
    )


def solution(mesh):
    in_specs = (
        P(("groups", "pool"), "sub"),
        P(("groups", "pool"), None, "sub"),
        P(("groups", "pool"), None, None, "sub"),
        P(("groups", "pool")),
        P("pool", "sub"),
        P(("groups", "pool", "sub"), None),
        P(),
        P(),
        P(("groups", "pool", "sub"), None),
        P("pool", None, "sub"),
        P("pool", None, "sub"),
        P("pool", "sub", None),
    )
    out_specs = P(("groups", "pool", "sub"), None)
    sizes = dict(mesh.shape)
    fused = sizes["pool"] == 16 and sizes["sub"] == 1
    return jax.shard_map(
        fused_device if fused else per_device, mesh=mesh, in_specs=in_specs, out_specs=out_specs, check_vma=False
    )
```

```python
import functools

import jax
import jax.numpy as jnp
from jax import lax
from jax.experimental import pallas as pl
from jax.experimental.pallas import tpu as pltpu
from jax.sharding import PartitionSpec as P

QH = 64
KVH = 4
HEAD = 128
TOPK = 8


norm_eps = 1e-06


def attend(query, new_kv, kv_cache, lengths):
    rows_att = query.shape[0]
    cache_len = kv_cache.shape[1]
    groups = kv_cache.shape[3] // HEAD
    per_group = QH // KVH
    queries = query.reshape(rows_att, groups, per_group, HEAD)
    cached_keys = kv_cache[:, :, 0].reshape(rows_att, cache_len, groups, HEAD)
    cached_values = kv_cache[:, :, 1].reshape(rows_att, cache_len, groups, HEAD)
    new_key = new_kv[:, 0].reshape(rows_att, groups, HEAD)
    new_value = new_kv[:, 1].reshape(rows_att, groups, HEAD)
    score_scale = HEAD ** (-0.5)
    scores = (
        jnp.einsum("rgqd,rjgd->rgqj", queries, cached_keys, preferred_element_type=jnp.float32)
        * score_scale
    )
    own_score = (
        jnp.einsum("rgqd,rgd->rgq", queries, new_key, preferred_element_type=jnp.float32)
        * score_scale
    )
    visible = jnp.arange(cache_len, dtype=jnp.int32)[None, :] < lengths[:, None]
    scores = jnp.where(visible[:, None, None, :], scores, jnp.float32(-1e30))
    row_max = jnp.maximum(jnp.max(scores, axis=-1), own_score)
    weights = jnp.exp(scores - row_max[..., None])
    own_weight = jnp.exp(own_score - row_max)
    denominator = jnp.sum(weights, axis=-1) + own_weight
    attn_probs = (weights / denominator[..., None]).astype(jnp.bfloat16)
    own_prob = (own_weight / denominator).astype(jnp.bfloat16)
    attended = jnp.einsum(
        "rgqj,rjgd->rgqd", attn_probs, cached_values, preferred_element_type=jnp.float32
    )
    attended = (
        attended
        + own_prob.astype(jnp.float32)[..., None] * new_value.astype(jnp.float32)[:, :, None, :]
    )
    return attended.astype(jnp.bfloat16).reshape(rows_att, -1)


def per_device(
    query,
    new_kv,
    kv_cache,
    lengths,
    o_weight,
    residual,
    norm_gain,
    router_weight,
    expert_ids,
    gate_weight,
    up_weight,
    down_weight,
):
    pool_size = lax.axis_size("pool")
    sub_size = lax.axis_size("sub")
    rows_dev = residual.shape[0]
    width = residual.shape[1]
    col_count = o_weight.shape[0]
    experts = router_weight.shape[0]
    attended = attend(query, new_kv, kv_cache, lengths)
    partial_value = lax.dot_general(
        lax.all_gather(attended, "pool", axis=0, tiled=True),
        o_weight,
        (((1,), (1,)), ((), ())),
        preferred_element_type=jnp.float32,
    )
    exchanged = lax.all_to_all(
        partial_value.astype(jnp.bfloat16), ("pool", "sub"), split_axis=0, concat_axis=1, tiled=True
    ).astype(partial_value.dtype)
    projected = jnp.sum(
        exchanged.reshape(rows_dev, pool_size, sub_size, col_count), axis=2
    ).reshape(rows_dev, width)
    hidden = residual.astype(jnp.float32) + projected
    mean_square = jnp.mean(hidden * hidden, axis=-1, keepdims=True)
    normed = (hidden * lax.rsqrt(mean_square + norm_eps) * norm_gain.astype(jnp.float32)).astype(
        jnp.bfloat16
    )
    logits = lax.dot_general(
        normed, router_weight, (((1,), (1,)), ((), ())), preferred_element_type=jnp.float32
    )
    onehot = expert_ids[:, :, None] == jnp.arange(experts, dtype=jnp.int32)[None, None, :]
    chosen = jnp.sum(jnp.where(onehot, logits[:, None, :], 0.0), axis=2)
    raised = jnp.exp(chosen)
    route_weight = raised / jnp.sum(raised, axis=1, keepdims=True)
    weight_full = jnp.sum(jnp.where(onehot, route_weight[:, :, None], 0.0), axis=1)
    capacity = min(rows_dev, max(2, 2 * rows_dev * TOPK // pool_size))
    member = jnp.sum(onehot.astype(jnp.int32), axis=1)
    rank_in_block = jnp.cumsum(member, axis=0) - member
    slot_ids = jnp.arange(capacity, dtype=jnp.int32)
    selector = (member.T[:, None, :] == 1) & (
        rank_in_block.T[:, None, :] == slot_ids[None, :, None]
    )
    combine_coef = jnp.where(selector, weight_full.T[:, None, :], 0.0)
    selector_bf = selector.astype(jnp.bfloat16)
    sending = jnp.einsum(
        "emr,rd->emd", selector_bf, normed, preferred_element_type=jnp.float32
    ).astype(jnp.bfloat16)
    doubled = jnp.broadcast_to(sending[:, None], (experts, sub_size, capacity, width)).reshape(
        experts * sub_size, capacity, width
    )
    arrived = lax.all_to_all(doubled, ("pool", "sub"), split_axis=0, concat_axis=0, tiled=True)
    item_count = arrived.shape[-2]
    flat_rows = arrived.reshape(-1, arrived.shape[-1])
    gate_proj = jnp.dot(flat_rows, gate_weight[0], preferred_element_type=jnp.float32)
    up_proj = jnp.dot(flat_rows, up_weight[0], preferred_element_type=jnp.float32)
    inner_act = (jax.nn.silu(gate_proj) * up_proj).astype(jnp.bfloat16)
    half_out = jnp.dot(inner_act, down_weight[0], preferred_element_type=jnp.float32).astype(
        jnp.bfloat16
    )
    returned = lax.all_to_all(
        half_out.reshape(-1, item_count, half_out.shape[-1]),
        ("pool", "sub"),
        split_axis=0,
        concat_axis=0,
        tiled=True,
    )
    merged = jnp.sum(
        returned.reshape(experts, sub_size, capacity, width).astype(jnp.float32), axis=1
    )
    mixed = jnp.einsum("emr,emd->rd", combine_coef, merged, precision=lax.Precision.HIGHEST)
    return mixed.astype(jnp.bfloat16)


AG_CHUNKS = 2
RS_CHUNKS = 4
HID_CHUNKS = 2
hid_rows = 128 // HID_CHUNKS


def contract(a, b, dims):
    return lax.dot_general(a, b, ((dims[0], dims[1]), ((), ())), preferred_element_type=jnp.float32)


def fold(value):
    half = value.shape[1] // 2
    return jnp.concatenate([value[:, :half], value[:, half:]], axis=0)


def fused_kernel(
    query, new_kv, kv, lengths, o_weight, residual, norm_gain, router, expert_ids, gate, up, down,
    out,
    kv_v, o_v, gate_v, up_v, down_v, q_s, att_s, gathered, small_out, small_in, hid, gate_acc, up_acc,
    partial, sib_out, sib_in, x_out, x_in, z_out, z_in, own_sum,
    gain_row, load_sem, small_send, small_recv, ag_send, ag_recv, hid_send, hid_recv,
    sib_send, sib_recv, x_send, x_recv, z_send, z_recv,
):
    me = lax.axis_index("pool")
    core = lax.rem(me, 2)
    x = lax.rem(me // 2, 2)
    z = me // 4
    sibling = z * 4 + x * 2 + (1 - core)
    x_peer = z * 4 + (1 - x) * 2 + core

    def z_of(j):
        return (z, z + 1 - 2 * lax.rem(z, 2), z + 2 - 4 * (z // 2), 3 - z)[j]

    def same_x(j):
        return z_of(j) * 4 + x * 2 + core

    def other_x(j):
        return z_of(j) * 4 + (1 - x) * 2 + core

    def flip(index):
        return index - core + (1 - core)

    def remote(src, dst, send_sem, recv_sem, target):
        return pltpu.make_async_remote_copy(
            src_ref=src, dst_ref=dst, send_sem=send_sem, recv_sem=recv_sem,
            device_id={"pool": target}, device_id_type=pl.DeviceIdType.MESH,
        )

    barrier = pltpu.get_barrier_semaphore()
    for offset in range(1, 16):
        pl.semaphore_signal(
            barrier, inc=1, device_id={"pool": lax.rem(me + offset, 16)},
            device_id_type=pl.DeviceIdType.MESH,
        )

    loads = [
        pltpu.make_async_copy(kv.at[:, :, :, pl.ds(g * 128, 128)], kv_v.at[g], load_sem.at[g])
        for g in range(4)
    ]
    for at, (a, b) in enumerate(((o_weight, o_v), (gate, gate_v), (up, up_v), (down, down_v))):
        loads.append(pltpu.make_async_copy(a, b, load_sem.at[4 + at]))
    for load in loads[:4]:
        load.start()

    lane = lax.broadcasted_iota(jnp.int32, (8, 128), 1)
    member = jnp.zeros((8, 128), jnp.float32)
    for k in range(TOPK):
        member = member + (expert_ids[:, k : k + 1] == lane).astype(jnp.float32)
    member_pad = jnp.concatenate([member, jnp.zeros_like(member)], axis=0).astype(jnp.bfloat16)
    res = residual[...].astype(jnp.float32)
    for d in range(16):
        small_out[d, 0:16, :] = fold(res[:, d * 256 : (d + 1) * 256]).astype(jnp.bfloat16)
        small_out[d, 16:32, :] = member_pad
    small_in[me] = small_out[me]

    q_all = query[...].astype(jnp.float32)
    for h in range(QH):
        q_s[h] = q_all[:, h * 128 : (h + 1) * 128]

    def small_copy(offset):
        target = lax.rem(me + offset, 16)
        return remote(
            small_out.at[target], small_in.at[me], small_send.at[offset], small_recv.at[me], target
        )

    def small_arrival(offset):
        source = lax.rem(me + offset, 16)
        return remote(
            small_out.at[source], small_in.at[source], small_send.at[offset], small_recv.at[source], source
        )

    kv_rows = kv_v.reshape(4, 8, 256, 128)
    score_scale = HEAD ** (-0.5)
    position = lax.broadcasted_iota(jnp.int32, (16, 256), 1)
    is_key = lax.rem(position, 2) == 0
    position = position // 2

    def attend_group(g, slot):
        queries = [q_s[pl.ds(g * 16, 16), r, :] for r in range(8)]
        fresh = [new_kv[r, :, g * 128 : (g + 1) * 128].astype(jnp.float32) for r in range(8)]
        scores = [
            jnp.where(
                is_key & (position < lengths[r]),
                contract(queries[r].astype(jnp.bfloat16), kv_rows[g, r], ((1,), (1,))) * score_scale,
                jnp.float32(-1e30),
            )
            for r in range(8)
        ]
        scores = jnp.concatenate(scores, axis=0)
        keys = jnp.concatenate([jnp.broadcast_to(f[0:1], (16, 128)) for f in fresh], axis=0)
        own = jnp.sum(jnp.concatenate(queries, axis=0) * keys, axis=1, keepdims=True) * score_scale
        top = jnp.maximum(jnp.max(scores, axis=1, keepdims=True), own)
        weights = jnp.exp(scores - top)
        own_weight = jnp.exp(own - top)
        scale = 1.0 / (jnp.sum(weights, axis=1, keepdims=True) + own_weight)
        probs = pltpu.roll(weights * scale, 1, 1).astype(jnp.bfloat16)
        own_prob = (own_weight * scale).astype(jnp.bfloat16).astype(jnp.float32)
        results = [
            contract(probs[r * 16 : (r + 1) * 16], kv_rows[g, r], ((1,), (0,)))
            + own_prob[r * 16 : (r + 1) * 16] * fresh[r][1:2]
            for r in range(8)
        ]
        for r in range(8):
            att_s[pl.ds(slot * 16, 16), r, :] = results[r]

    def gather_ops(buf, send_sem, recv_sem):
        def send(source, target, n):
            return remote(buf.at[source], buf.at[source], send_sem.at[n], recv_sem.at[source], target)

        own = [send(me, same_x(j), j - 1) for j in (1, 2, 3)]
        own += [send(me, x_peer, 3), send(me, sibling, 4)]

        def arrive(source):
            send(source, sibling, 0).wait_recv()

        def relay_z(j):
            arrive(same_x(j))
            a = send(same_x(j), x_peer, 3 + 2 * j)
            b = send(same_x(j), sibling, 4 + 2 * j)
            a.start()
            b.start()

        def relay_x(j):
            arrive(other_x(j))
            send(other_x(j), sibling, 11 + j).start()

        def finish():
            for n in range(15):
                send(me, sibling, n).wait_send()

        return own, arrive, relay_z, relay_x, finish

    rings = [
        gather_ops(gathered.at[k], ag_send.at[k], ag_recv.at[k]) for k in range(AG_CHUNKS)
    ]
    for k in range(AG_CHUNKS):
        for gg in range(2):
            loads[2 * k + gg].wait()
        if k == 0:
            for load in loads[4:]:
                load.start()
        for gg in range(2):
            attend_group(2 * k + gg, gg)
        for h in range(16):
            gathered[k, me, :, h * 128 : (h + 1) * 128] = jnp.concatenate(
                [att_s[h], att_s[16 + h]], axis=0
            ).astype(jnp.bfloat16)
        if k == 0:
            pl.semaphore_wait(barrier, 15)
        for copy in rings[k][0]:
            copy.start()
        if k == 0:
            for offset in range(1, 16):
                small_copy(offset).start()

    for ring in rings:
        for j in (1, 2, 3):
            ring[2](j)
    for ring in rings:
        for j in (0, 1, 2, 3):
            ring[3](j)
    loads[4].wait()
    total = jnp.zeros((128, 256), jnp.float32)
    for k in range(AG_CHUNKS):
        own, arrive, relay_z, relay_x, finish = rings[k]
        for j in range(4):
            arrive(flip(same_x(j)))
            arrive(flip(other_x(j)))
        left = gathered[k].reshape(256, 2048)
        for gg in range(2):
            first = k * 4096 + gg * 2048
            product = contract(left, o_v[:, first : first + 2048], ((1,), (1,)))
            total = total + product.reshape(16, 2, 8, 256)[:, gg].reshape(128, 256)

    for offset in range(1, 16):
        small_arrival(offset).wait_recv()
    pieces = small_in[:, 0:16, :].astype(jnp.float32).reshape(16, 2, 8, 128)
    res_part = jnp.concatenate(
        [pieces[:, 0].reshape(128, 128), pieces[:, 1].reshape(128, 128)], axis=1
    )
    gain_row[...] = norm_gain[...].reshape(1, 4096).astype(jnp.float32)
    hidden = (total + res_part).astype(jnp.bfloat16)
    hid_rings = [gather_ops(hid.at[k], hid_send.at[k], hid_recv.at[k]) for k in range(HID_CHUNKS)]
    for k in range(HID_CHUNKS):
        hid[k, me] = hidden[k * hid_rows : (k + 1) * hid_rows]
        for copy in hid_rings[k][0]:
            copy.start()
    loads[5].wait()
    loads[6].wait()
    for ring in hid_rings:
        for j in (1, 2, 3):
            ring[2](j)

    def project(pair, state, first=False):
        square, logits = state
        gate_sum = up_sum = None
        for t in range(2):
            s = pair * 2 + t
            at = pl.ds(pl.multiple_of(s * 256, 256), 256)
            h = jnp.concatenate([hid[k, s] for k in range(HID_CHUNKS)], axis=0).astype(jnp.float32)
            square = square + jnp.sum(h * h, axis=1, keepdims=True)
            scaled = (h * gain_row[:, at]).astype(jnp.bfloat16)
            logits = logits + contract(scaled, router[:, at], ((1,), (1,)))
            a = contract(scaled, gate_v[at, :], ((1,), (0,)))
            b = contract(scaled, up_v[at, :], ((1,), (0,)))
            gate_sum = a if gate_sum is None else gate_sum + a
            up_sum = b if up_sum is None else up_sum + b
        if first:
            gate_acc[...] = gate_sum
            up_acc[...] = up_sum
        else:
            gate_acc[...] += gate_sum
            up_acc[...] += up_sum
        return square, logits

    state = (jnp.zeros((128, 1), jnp.float32), jnp.zeros((128, 16), jnp.float32))
    for j in range(4):
        for ring in hid_rings:
            ring[1](flip(same_x(j)))
        state = project(z_of(j) * 2 + x, state, first=j == 0)
        for ring in hid_rings:
            ring[3](j)
    for j in range(4):
        for ring in hid_rings:
            ring[1](flip(other_x(j)))
        state = project(z_of(j) * 2 + (1 - x), state)
    square, logits = state
    inv = lax.rsqrt(square * (1.0 / 4096) + norm_eps)
    logits = logits * inv
    members = small_in[:, 16:32, :].astype(jnp.float32)[:, 0:8, :].reshape(128, 128)[:, 0:16]
    raised = jnp.where(members > 0.5, jnp.exp(logits), 0.0)
    mine = lax.broadcasted_iota(jnp.int32, (128, 16), 1) == me
    coef = jnp.sum(jnp.where(mine, raised, 0.0), axis=1, keepdims=True) / jnp.sum(
        raised, axis=1, keepdims=True
    )
    gate_proj = gate_acc[...] * inv
    inner = (gate_proj / (1.0 + jnp.exp(-gate_proj)) * (up_acc[...] * inv)).astype(jnp.bfloat16)
    loads[7].wait()

    width = 4096 // RS_CHUNKS

    def sib_copy(n):
        return remote(sib_out.at[n], sib_in.at[n], sib_send.at[n], sib_recv.at[n], sibling)

    def x_copy(n):
        return remote(x_out.at[n], x_in.at[n], x_send.at[n], x_recv.at[n], x_peer)

    def z_copy(n, j):
        return remote(
            z_out.at[n, j - 1], z_in.at[n, j - 1], z_send.at[n, j - 1], z_recv.at[n, j - 1], same_x(j)
        )

    def stage_down(n):
        product = contract(inner, down_v[:, n * width : (n + 1) * width], ((1,), (0,))) * coef
        partial[n] = product.reshape(16, 8, width)
        for chip in range(8):
            sib_out[n, chip] = fold(partial[n, chip * 2 + (1 - core)]).astype(jnp.bfloat16)
        sib_copy(n).start()

    def chip_sum(n, chip):
        return fold(partial[n, chip * 2 + core]) + sib_in[n, chip].astype(jnp.float32)

    def stage_x(n):
        sib_copy(n).wait_recv()
        for zz in range(4):
            x_out[n, zz] = chip_sum(n, zz * 2 + (1 - x)).astype(jnp.bfloat16)
        x_copy(n).start()

    def stage_z(n):
        x_copy(n).wait_recv()
        for j in range(4):
            total = chip_sum(n, z_of(j) * 2 + x) + x_in[n, z_of(j)].astype(jnp.float32)
            if j:
                z_out[n, j - 1] = total.astype(jnp.bfloat16)
                z_copy(n, j).start()
            else:
                own_sum[n] = total

    def stage_end(n):
        total = own_sum[n]
        for j in (1, 2, 3):
            z_copy(n, j).wait_recv()
            total = total + z_in[n, j - 1].astype(jnp.float32)
        out[:, n * width : (n + 1) * width] = jnp.concatenate(
            [total[0:8], total[8:16]], axis=1
        ).astype(jnp.bfloat16)

    for stage in (stage_down, stage_x, stage_z, stage_end):
        for n in range(RS_CHUNKS):
            stage(n)

    for offset in range(1, 16):
        small_copy(offset).wait_send()
    for ring in rings:
        ring[4]()
    for ring in hid_rings:
        ring[4]()
    for n in range(RS_CHUNKS):
        sib_copy(n).wait_send()
        x_copy(n).wait_send()
        for j in (1, 2, 3):
            z_copy(n, j).wait_send()


def fused_device(
    query, new_kv, kv_cache, lengths, o_weight, residual, norm_gain, router_weight, expert_ids,
    gate_weight, up_weight, down_weight,
):
    bf16, f32 = jnp.bfloat16, jnp.float32
    dma = pltpu.SemaphoreType.DMA
    half = 4096 // RS_CHUNKS // 2
    vmem = pl.BlockSpec(memory_space=pltpu.VMEM)
    smem = pl.BlockSpec(memory_space=pltpu.SMEM)
    hbm = pl.BlockSpec(memory_space=pl.ANY)
    return pl.pallas_call(
        fused_kernel,
        out_shape=jax.ShapeDtypeStruct((8, 4096), bf16),
        in_specs=[vmem, vmem, hbm, smem, hbm, vmem, vmem, vmem, vmem, hbm, hbm, hbm],
        out_specs=vmem,
        scratch_shapes=[
            pltpu.VMEM((4, 8, 128, 2, 128), bf16),
            pltpu.VMEM((256, 8192), bf16),
            pltpu.VMEM((4096, 768), bf16),
            pltpu.VMEM((4096, 768), bf16),
            pltpu.VMEM((768, 4096), bf16),
            pltpu.VMEM((64, 8, 128), f32),
            pltpu.VMEM((32, 8, 128), f32),
            pltpu.VMEM((AG_CHUNKS, 16, 16, 2048), bf16),
            pltpu.VMEM((16, 32, 128), bf16),
            pltpu.VMEM((16, 32, 128), bf16),
            pltpu.VMEM((HID_CHUNKS, 16, hid_rows, 256), bf16),
            pltpu.VMEM((128, 768), f32),
            pltpu.VMEM((128, 768), f32),
            pltpu.VMEM((RS_CHUNKS, 16, 8, 2 * half), f32),
            pltpu.VMEM((RS_CHUNKS, 8, 16, half), bf16),
            pltpu.VMEM((RS_CHUNKS, 8, 16, half), bf16),
            pltpu.VMEM((RS_CHUNKS, 4, 16, half), bf16),
            pltpu.VMEM((RS_CHUNKS, 4, 16, half), bf16),
            pltpu.VMEM((RS_CHUNKS, 3, 16, half), bf16),
            pltpu.VMEM((RS_CHUNKS, 3, 16, half), bf16),
            pltpu.VMEM((RS_CHUNKS, 16, half), f32),
            pltpu.VMEM((1, 4096), f32),
            dma((8,)),
            dma((16,)),
            dma((16,)),
            dma((AG_CHUNKS, 15)),
            dma((AG_CHUNKS, 16)),
            dma((HID_CHUNKS, 15)),
            dma((HID_CHUNKS, 16)),
            dma((RS_CHUNKS,)),
            dma((RS_CHUNKS,)),
            dma((RS_CHUNKS,)),
            dma((RS_CHUNKS,)),
            dma((RS_CHUNKS, 3)),
            dma((RS_CHUNKS, 3)),
        ],
        compiler_params=pltpu.CompilerParams(
            collective_id=0, has_side_effects=True, vmem_limit_bytes=56 * 1024 * 1024
        ),
        cost_estimate=pl.CostEstimate(
            flops=3_500_000_000, bytes_accessed=27_000_000, transcendentals=300_000
        ),
    )(
        query, new_kv, kv_cache, lengths, o_weight, residual, norm_gain, router_weight,
        expert_ids, gate_weight[0], up_weight[0], down_weight[0],
    )


def solution(mesh):
    in_specs = (
        P(("groups", "pool"), "sub"),
        P(("groups", "pool"), None, "sub"),
        P(("groups", "pool"), None, None, "sub"),
        P(("groups", "pool")),
        P("pool", "sub"),
        P(("groups", "pool", "sub"), None),
        P(),
        P(),
        P(("groups", "pool", "sub"), None),
        P("pool", None, "sub"),
        P("pool", None, "sub"),
        P("pool", "sub", None),
    )
    out_specs = P(("groups", "pool", "sub"), None)
    sizes = dict(mesh.shape)
    fused = sizes["pool"] == 16 and sizes["sub"] == 1
    return jax.shard_map(
        fused_device if fused else per_device, mesh=mesh, in_specs=in_specs, out_specs=out_specs, check_vma=False
    )
```
